256 devices in a mesh: row: 8 (over z_hi, core), col: 32 (over y, x, z_lo).
Axes of the slice: x: 4, y: 4, z: 8 (z_hi: 4, z_lo: 2; z = z_hi * 2 + z_lo), core: 2. Of those that a mesh axis runs over, the one named last changes fastest.
Arguments:
- matrix: bfloat16 [6144, 6144], P('col', 'row'), as said below
- pattern: int32 [48, 48], replicated, may hold values 0 or 1
- shift: float32 [6144], replicated, may hold values from 0.25 to 1
Outputs:
- square: bfloat16 [6144, 6144], P('col', 'row')
- updated: bfloat16 [6144, 6144], P('col', 'row')
The draws below stay inside these ranges and needn't reach their ends.
Inputs may be any that keep to these rules, and one draw needn't show every extreme that they name: matrix is symmetric: the entry in row i and column j equals the entry in row j and column i.
All inputs are finite; a program needn't handle non-finite values.
Results may differ from the reference program's by a relative error of at most 0.0052.
Values may be sent and summed in bfloat16 or wider, within the bound.
A program may use at most 64 MiB of HBM per device.

```python
import math
import jax
import jax.numpy as jnp

BLOCK = 128
ORDER = 6144
NBLK = 48


def block_gains(gain_key, count, low, high, power):
    ramp = 1.0 + 2.0 * jnp.arange(count, dtype=jnp.float32) / (count - 1)
    spread = jax.random.uniform(gain_key, (count,), jnp.float32, math.log(low), math.log(high))
    return jnp.exp(spread) * ramp ** power


def draw_matrix(key, part):
    key = jax.random.fold_in(key, 11)
    noise_key, gain_key, common_key = jax.random.split(key, 3)
    count = ORDER // BLOCK
    noise = jax.random.normal(noise_key, (ORDER, ORDER), jnp.float32)
    gains = block_gains(gain_key, count, 0.5623413, 1.7782794, 0.25)
    common = jnp.exp(jax.random.uniform(common_key, (), jnp.float32, math.log(0.7), math.log(1.4)))
    symmetric = jnp.clip((noise + noise.T) * 0.70710678, -4.0, 4.0)
    scales = jnp.repeat(gains, BLOCK)
    values = symmetric * scales[:, None] * scales[None, :] * (common / math.sqrt(BLOCK))
    return values.astype(jnp.bfloat16)


def with_ends(entries, stream_key, least, largest):
    longest = entries.shape.index(max(entries.shape))
    spots = []
    for shift in (0, 1):
        where = [jax.random.randint(jax.random.fold_in(stream_key, axis), (), 0, length) for axis, length in enumerate(entries.shape)]
        where[longest] = (where[longest] + shift) % entries.shape[longest]
        spots.append(tuple(where))
    return entries.at[spots[0]].set(least).at[spots[1]].set(largest)


def setup_inputs(seed: int = 0) -> dict:
    streams_of = jax.random.split(jax.random.key(seed), 4)
    return {
        "matrix": draw_matrix(jax.random.fold_in(streams_of[3], 71), 0),
        "pattern": with_ends((jax.random.randint(streams_of[1], (NBLK, NBLK), 0, 4) < 1).astype(jnp.int32), jax.random.fold_in(streams_of[1], 1), 0, 1),
        "shift": jnp.clip(jnp.exp(jax.random.uniform(streams_of[2], (ORDER,), jnp.float32, math.log(0.25), math.log(1.0))), 0.25, 1.0),
    }


def reference(matrix, pattern, shift):
    count = pattern.shape[0]
    blocks = jnp.maximum(pattern, jnp.eye(count, dtype=jnp.int32))
    keep = jnp.repeat(jnp.repeat(blocks, BLOCK, 0), BLOCK, 1) > 0
    iterate = (jnp.where(keep, matrix.astype(jnp.float32), 0.0) + jnp.diag(shift)).astype(jnp.bfloat16)
    full = jnp.where(keep, jnp.dot(iterate, iterate, preferred_element_type=jnp.float32), 0.0)
    trace = jnp.sum(jnp.diagonal(full))
    square = full.astype(jnp.bfloat16)
    gamma = jnp.sqrt(ORDER / jnp.maximum(jnp.abs(trace), 1.0))
    cube = jnp.where(keep, jnp.dot(iterate, square, preferred_element_type=jnp.float32), 0.0)
    updated = (1.5 * gamma * iterate.astype(jnp.float32) - 0.5 * gamma ** 3 * cube).astype(jnp.bfloat16)
    return (square, updated)
```

```python
import jax
import jax.numpy as jnp
from jax import lax
from jax.experimental import pallas as pl
from jax.experimental.pallas import tpu as pltpu
from jax.sharding import PartitionSpec as P

BLOCK = 128
ORDER = 6144
NBLK = 48
ROWS = 192
COLS = 768
SUB = 64
CHUNK = 256
NCH = COLS // CHUNK
DEPTH = 8 * ROWS
MESH = pl.DeviceIdType.MESH
F32 = jnp.float32
BF16 = jnp.bfloat16


def kernel(m_ref, pat_ref, shift_ref, sq_ref, up_ref,
           g1, g2, zbuf, lhs, part1, part2, got1, got2, acc, tsend, trecv, ssem, rsem, lsem):
    r = lax.axis_index("row")
    c = lax.axis_index("col")
    zhi, core = r // 2, r % 2
    y, x, zlo = c // 8, (c // 2) % 4, c % 2
    me = c % 8

    def dev(dx=0, dy=0, flip=0, dz=0, other=0):
        xx, yy, zz = (x + dx + 4) % 4, (y + dy + 4) % 4, (zhi + dz + 4) % 4
        zl = 1 - zlo if flip else zlo
        cc = 1 - core if other else core
        return (zz * 2 + cc, (yy * 4 + xx) * 2 + zl)

    def place(dx, flip):
        return ((x + dx + 4) % 4) * 2 + (1 - zlo if flip else zlo)

    def rows(slot, start=0, size=ROWS):
        return pl.ds(pl.multiple_of(slot * ROWS + start, 16), size)

    barrier = pltpu.get_barrier_semaphore()
    partners = [dev(dx=1), dev(dx=-1), dev(dy=1), dev(dy=-1), dev(dy=2),
                dev(dz=1), dev(dz=-1), dev(flip=1), dev(other=1)]
    for p in partners:
        pl.semaphore_signal(barrier, inc=1, device_id=p, device_id_type=MESH)

    terms = jnp.zeros((SUB, BLOCK), F32)
    keeps = {}
    for s in range(ROWS // SUB):
        br = (3 * c + s) // 2
        for t in range(COLS // BLOCK):
            bc = 6 * r + t
            diag = br == bc
            keep = jnp.where((pat_ref[br, bc] > 0) | diag, 1.0, 0.0).astype(F32)
            keep_t = jnp.where((pat_ref[bc, br] > 0) | diag, 1.0, 0.0).astype(F32)
            keeps[s, t] = keep
            m = m_ref[s * SUB:(s + 1) * SUB, t * BLOCK:(t + 1) * BLOCK].astype(F32)
            row_ids = c * ROWS + s * SUB + lax.broadcasted_iota(jnp.int32, (SUB, BLOCK), 0)
            col_ids = r * COLS + t * BLOCK + lax.broadcasted_iota(jnp.int32, (SUB, BLOCK), 1)
            on = jnp.where(row_ids == col_ids, shift_ref[pl.ds(bc, 1), :], 0.0)
            a = (m * keep + on).astype(BF16)
            a_t = (m * keep_t + on).astype(BF16)
            terms += a.astype(F32) * a_t.astype(F32)
            k, lane = t // 2, (t % 2) * BLOCK
            g1[k, rows(me, s * SUB, SUB), lane:lane + BLOCK] = a
            zbuf[zhi, s * SUB:(s + 1) * SUB, t * BLOCK:(t + 1) * BLOCK] = a
    tsend[0] = jnp.sum(terms.reshape(SUB // 8, 8, BLOCK), axis=0)

    pl.semaphore_wait(barrier, len(partners))

    index = {}
    started = []

    def number(key):
        if key not in index:
            index[key] = len(index)
        return index[key]

    def copy(key, src, dst, to):
        n = number(key)
        return pltpu.make_async_remote_copy(
            src_ref=src, dst_ref=dst, send_sem=ssem.at[n], recv_sem=rsem.at[n],
            device_id=to, device_id_type=MESH)

    def start(key, src, dst, to):
        op = copy(key, src, dst, to)
        op.start()
        started.append(op)

    def arrived(key, dst):
        copy(key, dst, dst, dev(other=1)).wait_recv()

    def own(g, name, k):
        mine = g.at[k, rows(me), :]
        start((name, "zp", k), mine, mine, dev(flip=1))
        start((name, "xp", k), mine, mine, dev(dx=1))
        start((name, "xm", k), mine, mine, dev(dx=-1))

    def pair(g, name, k):
        ref = g.at[k, rows(place(0, 1)), :]
        arrived((name, "zp", k), ref)
        start((name, "fp", k), ref, ref, dev(dx=1))
        start((name, "fm", k), ref, ref, dev(dx=-1))

    def far(g, name, k, flip):
        first, second = ("fp", "fm") if flip else ("xp", "xm")
        arrived((name, first, k), g.at[k, rows(place(-1, flip)), :])
        ref = g.at[k, rows(place(-1, flip), 0, ROWS // 2), :]
        start((name, "hp", flip, k), ref, ref, dev(dx=1))
        arrived((name, second, k), g.at[k, rows(place(1, flip)), :])
        ref = g.at[k, rows(place(1, flip), ROWS // 2, ROWS // 2), :]
        start((name, "hm", flip, k), ref, ref, dev(dx=-1))

    def last(g, name, k, flip):
        slot = place(2, flip)
        arrived((name, "hp", flip, k), g.at[k, rows(slot, 0, ROWS // 2), :])
        arrived((name, "hm", flip, k), g.at[k, rows(slot, ROWS // 2, ROWS // 2), :])

    half = SUB // 2

    def along_z(q):
        ref = zbuf.at[zhi, pl.ds(q * SUB, SUB), :]
        start(("z+", q), ref, ref, dev(dz=1))
        start(("z-", q), ref, ref, dev(dz=-1))

    def relay_z(q, up):
        if up:
            slot = (zhi + 3) % 4
            arrived(("z+", q), zbuf.at[slot, pl.ds(q * SUB, SUB), :])
            ref = zbuf.at[slot, pl.ds(q * SUB, half), :]
            start(("zz+", q), ref, ref, dev(dz=1))
        else:
            slot = (zhi + 1) % 4
            arrived(("z-", q), zbuf.at[slot, pl.ds(q * SUB, SUB), :])
            ref = zbuf.at[slot, pl.ds(q * SUB + half, half), :]
            start(("zz-", q), ref, ref, dev(dz=-1))

    def relay_last(q):
        slot = (zhi + 2) % 4
        arrived(("zz+", q), zbuf.at[slot, pl.ds(q * SUB, half), :])
        arrived(("zz-", q), zbuf.at[slot, pl.ds(q * SUB + half, half), :])

    core_cols = pl.ds(pl.multiple_of(core * COLS, COLS), COLS)
    sent_y = []

    def along_y(dz, q):
        slot = (zhi + dz + 4) % 4
        d = (slot - y + 4) % 4
        n = number(("ly", dz, q))
        src = zbuf.at[slot, pl.ds(q * SUB, SUB), :]
        dst = lhs.at[rows(y, q * SUB, SUB), core_cols]

        def op():
            return pltpu.make_async_remote_copy(
                src_ref=src, dst_ref=dst, send_sem=ssem.at[n],
                recv_sem=lsem.at[(d + 3) % 4, q],
                device_id=(r, (slot * 4 + x) * 2 + zlo), device_id_type=MESH)

        @pl.when(d != 0)
        def _():
            op().start()

        @pl.when(d == 0)
        def _():
            lhs[rows(y, q * SUB, SUB), core_cols] = zbuf[slot, q * SUB:(q + 1) * SUB, :]

        sent_y.append((d, op))

    def to_core(d):
        slot = (y - d + 4) % 4
        if d:
            for q in range(3):
                ref = lhs.at[rows(slot, q * SUB, SUB), core_cols]
                pltpu.make_async_remote_copy(
                    src_ref=ref, dst_ref=ref, send_sem=ssem.at[0], recv_sem=lsem.at[d - 1, q],
                    device_id=dev(other=1), device_id_type=MESH).wait_recv()
        ref = lhs.at[rows(slot), core_cols]
        start(("lc", d), ref, ref, dev(other=1))

    def from_core(d):
        slot = (y - d + 4) % 4
        cols = pl.ds(pl.multiple_of((1 - core) * COLS, COLS), COLS)
        arrived(("lc", d), lhs.at[rows(slot), cols])

    odd_x, odd_z, odd_y = x % 2, zhi % 2, y % 2
    trace_to = [
        dev(other=1), dev(flip=1),
        dev(dx=1 - 2 * odd_x), dev(dx=2 * odd_x - 1),
        dev(dy=1 - 2 * odd_y), dev(dy=2 * odd_y - 1),
        dev(dz=1 - 2 * odd_z), dev(dz=2 * odd_z - 1),
    ]

    def trace_send(i):
        start(("t", i), tsend.at[i], trecv.at[i], trace_to[i])

    def trace_sum(i):
        arrived(("t", i), trecv.at[i])
        tsend[i + 1] = tsend[i] + trecv[i]
        if i + 1 < len(trace_to):
            trace_send(i + 1)

    def product(g, part, name, k):
        acc[...] = jnp.dot(lhs[...], g[k], preferred_element_type=F32)
        part[k] = acc[...].astype(BF16)
        for d in (2, 1, 3):
            start((name, "rs", d, k), part.at[k, rows((y + d) % 4), :],
                  (got1 if name == "a" else got2).at[k, d - 1], dev(dy=d))

    def total(got, name, k, mine):
        for d in (1, 3, 2):
            arrived((name, "rs", d, k), got.at[k, d - 1])
        return mine + (got[k, 0].astype(F32) + got[k, 2].astype(F32)) + got[k, 1].astype(F32)

    for k in range(NCH):
        own(g1, "a", k)
        along_z(k)
    for q in range(3):
        along_y(0, q)
    trace_send(0)
    for k in range(NCH):
        pair(g1, "a", k)
        far(g1, "a", k, 0)
        relay_z(k, True)
        relay_z(k, False)
        along_y(-1, k)
        along_y(1, k)
    trace_sum(0)
    for k in range(NCH):
        far(g1, "a", k, 1)
    trace_sum(1)
    for q in range(3):
        relay_last(q)
        along_y(2, q)
    trace_sum(2)
    for d in (0, 1, 3, 2):
        to_core(d)
    for k in range(NCH):
        last(g1, "a", k, 0)
        last(g1, "a", k, 1)
    for d in (0, 1, 3, 2):
        from_core(d)

    def mine():
        return acc[rows(y), :]

    held = []
    for k in range(NCH):
        product(g1, part1, "a", k)
        held.append(mine())
    trace_sum(3)
    for k in range(NCH):
        full = total(got1, "a", k, held[k])
        for s in range(ROWS // SUB):
            for h in range(2):
                t = 2 * k + h
                piece = full[s * SUB:(s + 1) * SUB, h * BLOCK:(h + 1) * BLOCK] * keeps[s, t]
                piece = piece.astype(BF16)
                g2[k, rows(me, s * SUB, SUB), h * BLOCK:(h + 1) * BLOCK] = piece
                sq_ref[s * SUB:(s + 1) * SUB, t * BLOCK:(t + 1) * BLOCK] = piece
        own(g2, "b", k)
        if k:
            pair(g2, "b", k - 1)
            far(g2, "b", k - 1, 0)
    trace_sum(4)
    pair(g2, "b", NCH - 1)
    far(g2, "b", 0, 1)
    far(g2, "b", NCH - 1, 0)
    trace_sum(5)
    far(g2, "b", 1, 1)
    last(g2, "b", 0, 0)
    last(g2, "b", 0, 1)
    held = []
    product(g2, part2, "b", 0)
    held.append(mine())
    trace_sum(6)
    far(g2, "b", 2, 1)
    last(g2, "b", 1, 0)
    last(g2, "b", 1, 1)
    product(g2, part2, "b", 1)
    held.append(mine())
    trace_sum(7)
    last(g2, "b", 2, 0)
    last(g2, "b", 2, 1)
    product(g2, part2, "b", 2)
    held.append(mine())

    trace = jnp.sum(tsend[len(trace_to)], keepdims=True)
    gamma = jnp.sqrt(ORDER / jnp.maximum(jnp.abs(trace), 1.0))
    lead, tail = 1.5 * gamma, 0.5 * gamma * gamma * gamma
    for k in range(NCH):
        cube = total(got2, "b", k, held[k])
        for s in range(ROWS // SUB):
            for h in range(2):
                t = 2 * k + h
                piece = cube[s * SUB:(s + 1) * SUB, h * BLOCK:(h + 1) * BLOCK] * keeps[s, t]
                a = zbuf[zhi, s * SUB:(s + 1) * SUB, t * BLOCK:(t + 1) * BLOCK].astype(F32)
                up_ref[s * SUB:(s + 1) * SUB, t * BLOCK:(t + 1) * BLOCK] = (
                    lead * a - tail * piece).astype(BF16)

    for op in started:
        op.wait_send()
    for d, op in sent_y:
        @pl.when(d != 0)
        def _(op=op):
            op().wait_send()


NSEM = 128


def body(matrix, pattern, shift):
    block = jax.ShapeDtypeStruct((ROWS, COLS), BF16)
    vmem = pl.BlockSpec(memory_space=pltpu.VMEM)
    return pl.pallas_call(
        kernel,
        out_shape=(block, block),
        in_specs=[vmem, pl.BlockSpec(memory_space=pltpu.SMEM), vmem],
        out_specs=(vmem, vmem),
        scratch_shapes=[
            pltpu.VMEM((NCH, DEPTH, CHUNK), BF16),
            pltpu.VMEM((NCH, DEPTH, CHUNK), BF16),
            pltpu.VMEM((4, ROWS, COLS), BF16),
            pltpu.VMEM((4 * ROWS, DEPTH), BF16),
            pltpu.VMEM((NCH, 4 * ROWS, CHUNK), BF16),
            pltpu.VMEM((NCH, 4 * ROWS, CHUNK), BF16),
            pltpu.VMEM((NCH, 3, ROWS, CHUNK), BF16),
            pltpu.VMEM((NCH, 3, ROWS, CHUNK), BF16),
            pltpu.VMEM((4 * ROWS, CHUNK), F32),
            pltpu.VMEM((9, 8, BLOCK), F32),
            pltpu.VMEM((8, 8, BLOCK), F32),
            pltpu.SemaphoreType.DMA((NSEM,)),
            pltpu.SemaphoreType.DMA((NSEM,)),
            pltpu.SemaphoreType.DMA((3, 3)),
        ],
        compiler_params=pltpu.CompilerParams(
            collective_id=0, has_side_effects=True, vmem_limit_bytes=40 * 2**20),
        cost_estimate=pl.CostEstimate(
            flops=4 * ROWS * COLS * ORDER, bytes_accessed=6 * ROWS * COLS, transcendentals=0),
        name="sign_step",
    )(matrix, pattern, shift.reshape(NBLK, BLOCK))


def solution(mesh):
    placed = (P("col", "row"), P(), P())
    return jax.shard_map(
        body,
        mesh=mesh,
        in_specs=placed,
        out_specs=(P("col", "row"), P("col", "row")),
        check_vma=False,
    )
```

```python
import jax
import jax.numpy as jnp
from jax import lax
from jax.experimental import pallas as pl
from jax.experimental.pallas import tpu as pltpu
from jax.sharding import PartitionSpec as P

BLOCK = 128
ORDER = 6144
NBLK = 48
ROWS = 192
COLS = 768
WIDE = COLS // 2
SUB = 64
CHUNK = 256
NCH = COLS // CHUNK
DEPTH = 8 * ROWS
NQ = 2
PIECE = ROWS // NQ
NSEM = 80
MESH = pl.DeviceIdType.MESH
F32 = jnp.float32
BF16 = jnp.bfloat16


def kernel(m_ref, pat_ref, shift_ref, sq_ref, up_ref,
           g1, g2, zbuf, lhs, part1, part2, got1, got2, own1, own2, acc, tsend, trecv, sems):
    r = lax.axis_index("row")
    c = lax.axis_index("col")
    zhi, core = lax.div(r, 2), lax.rem(r, 2)
    y, x, zlo = lax.div(c, 8), lax.rem(lax.div(c, 2), 4), lax.rem(c, 2)
    me = y * 2 + zlo

    ys = {d: lax.rem(y + d, 4) for d in range(1, 4)}
    xs = {d: lax.rem(x + d, 4) for d in range(1, 4)}
    zs = {d: lax.rem(zhi + d, 4) for d in range(1, 4)}
    ys[0], xs[0], zs[0] = y, x, zhi
    y_up, y_down = (r, c + 8 * (ys[1] - y)), (r, c + 8 * (ys[3] - y))
    z_up, z_down = (r + 2 * (zs[1] - zhi), c), (r + 2 * (zs[3] - zhi), c)
    pair_dev = (r, c + 1 - 2 * zlo)
    core_dev = (r + 1 - 2 * core, c)
    x_dev = {d: (r, c + 2 * (xs[d] - x)) for d in range(1, 4)}

    def rows(slot, start=0, size=ROWS):
        return pl.ds(pl.multiple_of(slot * ROWS + start, 16), size)

    barrier = pltpu.get_barrier_semaphore()
    partners = [x_dev[1], x_dev[2], x_dev[3], y_up, y_down, z_up, z_down, pair_dev, core_dev]
    for p in partners:
        pl.semaphore_signal(barrier, inc=1, device_id=p, device_id_type=MESH)

    terms = jnp.zeros((SUB, BLOCK), F32)
    keeps = {}
    ahead = (lax.broadcasted_iota(jnp.int32, (SUB, BLOCK), 0)
             - lax.broadcasted_iota(jnp.int32, (SUB, BLOCK), 1))
    for s in range(ROWS // SUB):
        br = lax.div(3 * c + s, 2)
        for t in range(COLS // BLOCK):
            bc = 6 * r + t
            diag = br == bc
            keep = jnp.where((pat_ref[br, bc] > 0) | diag, 1.0, 0.0).astype(F32)
            keep_t = jnp.where((pat_ref[bc, br] > 0) | diag, 1.0, 0.0).astype(F32)
            keeps[s, t] = keep
            m = m_ref[s * SUB:(s + 1) * SUB, t * BLOCK:(t + 1) * BLOCK].astype(F32)
            gap = (r * COLS + t * BLOCK) - (c * ROWS + s * SUB)
            on = jnp.where(ahead == gap, shift_ref[pl.ds(bc, 1), :], 0.0)
            a = (m * keep + on).astype(BF16)
            a_t = (m * keep_t + on).astype(BF16)
            terms += a.astype(F32) * a_t.astype(F32)
            k, lane = t // 2, (t % 2) * BLOCK
            g1[k, rows(me, s * SUB, SUB), lane:lane + BLOCK] = a
            zbuf[zhi, t // 3, s * SUB:(s + 1) * SUB, (t % 3) * BLOCK:(t % 3 + 1) * BLOCK] = a
    tsend[0] = jnp.sum(terms.reshape(SUB // 8, 8, BLOCK), axis=0)

    pl.semaphore_wait(barrier, len(partners))

    index = {}

    def sem(key):
        if key not in index:
            index[key] = len(index)
        return sems.at[index[key]]

    def copy(out, into, src, dst, to):
        return pltpu.make_async_remote_copy(
            src_ref=src, dst_ref=dst, send_sem=sem(out), recv_sem=sem(into),
            device_id=to, device_id_type=MESH)

    def start(out, into, ref, to, dst=None):
        copy(out, into, ref, ref if dst is None else dst, to).start()

    def arrived(key, ref):
        copy(key, key, ref, ref, core_dev).wait_recv()

    def sent(key, ref):
        copy(key, key, ref, ref, core_dev).wait_send()

    slots = {(d, f): rows(ys[d] * 2 + (1 - zlo if f else zlo)) for d in range(4) for f in range(2)}
    tops = {(d, f): rows(ys[d] * 2 + (1 - zlo if f else zlo), 0, ROWS // 2)
            for d in range(4) for f in range(2)}
    ends = {(d, f): rows(ys[d] * 2 + (1 - zlo if f else zlo), ROWS // 2, ROWS // 2)
            for d in range(4) for f in range(2)}

    def own(g, name, k):
        ref = g.at[k, slots[0, 0], :]
        start((name, "out"), (name, "pair", k), ref, pair_dev)
        start((name, "out"), (name, "near", 0, k), ref, y_up)
        start((name, "out"), (name, "near", 0, k), ref, y_down)

    def pair(g, name, k):
        ref = g.at[k, slots[0, 1], :]
        arrived((name, "pair", k), ref)
        start((name, "out"), (name, "near", 1, k), ref, y_up)
        start((name, "out"), (name, "near", 1, k), ref, y_down)

    def near(g, name, k, f):
        arrived((name, "near", f, k), g.at[k, 0:2 * ROWS, :])

    def relay(g, name, k, f):
        near(g, name, k, f)
        start((name, "out"), (name, "far", f, k), g.at[k, tops[3, f], :], y_up)
        start((name, "out"), (name, "far", f, k), g.at[k, ends[1, f], :], y_down)

    def far(g, name, k, f):
        arrived((name, "far", f, k), g.at[k, slots[2, f], :])

    def far_pair(g, name, k):
        far(g, name, k, 0)
        start((name, "out"), (name, "far", 1, k), g.at[k, slots[2, 0], :], pair_dev)

    def along_z(q):
        ref = zbuf.at[zhi, :, q * PIECE:(q + 1) * PIECE, :]
        start(("z", "out"), ("z", q), ref, z_up)
        start(("z", "out"), ("z", q), ref, z_down)

    def relay_z(q):
        arrived(("z", q), zbuf.at[0:2, :, 0:PIECE, :])
        low, mid, high = q * PIECE, q * PIECE + PIECE // 2, (q + 1) * PIECE
        start(("z", "out"), ("zz", q), zbuf.at[zs[3], :, low:mid, :], z_up)
        start(("z", "out"), ("zz", q), zbuf.at[zs[1], :, mid:high, :], z_down)

    def relay_last(q):
        arrived(("zz", q), zbuf.at[zs[2], :, q * PIECE:(q + 1) * PIECE, :])

    direct = core == lax.div(x, 2)
    depth = {d: pl.ds(pl.multiple_of(zs[d] * WIDE, BLOCK), WIDE) for d in range(4)}
    to_x = [core * 2 + h for h in range(2)]
    home = lax.rem(x, 2)

    def along_x(d, q):
        dst = lhs.at[rows(x, q * PIECE, PIECE), depth[d]]
        for h in range(2):
            src = zbuf.at[zs[d], h, q * PIECE:(q + 1) * PIECE, :]

            @pl.when(to_x[h] != x)
            def _(h=h, src=src):
                start(("x", "out"), ("x", d), src, (r, c + 2 * (to_x[h] - x)), dst)

            @pl.when(to_x[h] == x)
            def _(h=h):
                lhs[rows(x, q * PIECE, PIECE), depth[d]] = zbuf[
                    zs[d], h, q * PIECE:(q + 1) * PIECE, :]

    def to_core(d):
        ref = lhs.at[:, depth[d]]

        @pl.when(direct)
        def _():
            arrived(("x", d), lhs.at[0:3 * ROWS, depth[d]])
            start(("core", "out"), ("core", d), ref, core_dev)

    def from_core(d):
        @pl.when(jnp.logical_not(direct))
        def _():
            arrived(("core", d), lhs.at[:, depth[d]])

    odd_x, odd_z, odd_y = lax.rem(x, 2), lax.rem(zhi, 2), lax.rem(y, 2)

    def step(first, d1, d3):
        return tuple(jnp.where(first, u, v) for u, v in zip(d1, d3))

    trace_to = [
        core_dev, pair_dev,
        step(odd_x == 0, x_dev[1], x_dev[3]), step(odd_x == 1, x_dev[1], x_dev[3]),
        step(odd_y == 0, y_up, y_down), step(odd_y == 1, y_up, y_down),
        step(odd_z == 0, z_up, z_down), step(odd_z == 1, z_up, z_down),
    ]

    def trace_send(i):
        start(("t", "out"), ("t", i), tsend.at[i], trace_to[i], trecv.at[i])

    def trace_sum(i):
        arrived(("t", i), trecv.at[i])
        tsend[i + 1] = tsend[i] + trecv[i]
        if i + 1 < len(trace_to):
            trace_send(i + 1)

    def part_dot(g, k, slot, first=False):
        term = jnp.dot(lhs[:, pl.ds(pl.multiple_of(slot * WIDE, BLOCK), WIDE)],
                       g[k, pl.ds(pl.multiple_of(slot * WIDE, 16), WIDE), :],
                       preferred_element_type=F32)
        acc[k] = term if first else acc[k] + term

    def ship(part, kept, got, name, k):
        for d in (2, 1, 3):
            part[k, d - 1] = acc[k, rows(xs[d]), :].astype(BF16)
        kept[k] = acc[k, rows(x), :]
        if k:
            sent((name, "sums out", k - 1), part.at[k - 1])
        for d in (2, 1, 3):
            start((name, "sums out", k), (name, "sums", k), part.at[k, d - 1], x_dev[d],
                  got.at[k, d - 1])

    def total(got, kept, name, k):
        arrived((name, "sums", k), got.at[k])
        return kept[k] + (got[k, 0].astype(F32) + got[k, 2].astype(F32)) + got[k, 1].astype(F32)

    for k in range(NCH):
        own(g1, "a", k)
    for q in range(NQ):
        along_x(0, q)
    trace_send(0)
    pair(g1, "a", 0)
    along_z(0)
    relay(g1, "a", 0, 0)
    pair(g1, "a", 1)
    along_z(1)
    relay(g1, "a", 1, 0)
    pair(g1, "a", 2)
    relay(g1, "a", 2, 0)
    relay_z(0)
    along_x(3, 0)
    along_x(1, 0)
    trace_sum(0)
    relay(g1, "a", 0, 1)
    relay_z(1)
    along_x(3, 1)
    along_x(1, 1)
    trace_sum(1)
    relay(g1, "a", 1, 1)
    relay(g1, "a", 2, 1)
    to_core(0)
    relay_last(0)
    along_x(2, 0)
    to_core(3)
    to_core(1)
    for k in range(NCH):
        far(g1, "a", k, 0)
        far(g1, "a", k, 1)
    for d in (0, 3, 1):
        from_core(d)
        if d == 3:
            relay_last(1)
            along_x(2, 1)
        for k in range(NCH):
            part_dot(g1, k, zs[d], d == 0)
    to_core(2)
    from_core(2)
    for k in range(NCH):
        part_dot(g1, k, zs[2])
        ship(part1, own1, got1, "a", k)
    def squares(k):
        full = total(got1, own1, "a", k)
        for s in range(ROWS // SUB):
            for h in range(2):
                t = 2 * k + h
                piece = full[s * SUB:(s + 1) * SUB, h * BLOCK:(h + 1) * BLOCK] * keeps[s, t]
                piece = piece.astype(BF16)
                g2[k, rows(me, s * SUB, SUB), h * BLOCK:(h + 1) * BLOCK] = piece
                sq_ref[s * SUB:(s + 1) * SUB, t * BLOCK:(t + 1) * BLOCK] = piece
        own(g2, "b", k)

    squares(0)
    trace_sum(2)
    pair(g2, "b", 0)
    relay(g2, "b", 0, 0)
    squares(1)
    trace_sum(3)
    far_pair(g2, "b", 0)
    pair(g2, "b", 1)
    relay(g2, "b", 1, 0)
    part_dot(g2, 0, ys[0], True)
    squares(2)
    trace_sum(4)
    near(g2, "b", 0, 1)
    part_dot(g2, 0, ys[1])
    part_dot(g2, 0, ys[3])
    far_pair(g2, "b", 1)
    part_dot(g2, 1, ys[0], True)
    pair(g2, "b", 2)
    relay(g2, "b", 2, 0)
    far(g2, "b", 0, 1)
    part_dot(g2, 0, ys[2])
    ship(part2, own2, got2, "b", 0)
    near(g2, "b", 1, 1)
    part_dot(g2, 1, ys[1])
    part_dot(g2, 1, ys[3])
    far_pair(g2, "b", 2)
    part_dot(g2, 2, ys[0], True)
    far(g2, "b", 1, 1)
    part_dot(g2, 1, ys[2])
    trace_sum(5)
    ship(part2, own2, got2, "b", 1)
    near(g2, "b", 2, 1)
    part_dot(g2, 2, ys[1])
    part_dot(g2, 2, ys[3])
    trace_sum(6)
    far(g2, "b", 2, 1)
    part_dot(g2, 2, ys[2])
    ship(part2, own2, got2, "b", 2)
    trace_sum(7)

    trace = jnp.sum(tsend[len(trace_to)], keepdims=True)
    gamma = jnp.sqrt(ORDER / jnp.maximum(jnp.abs(trace), 1.0))
    lead, tail = 1.5 * gamma, 0.5 * gamma * gamma * gamma
    for k in range(NCH):
        cube = total(got2, own2, "b", k)
        for s in range(ROWS // SUB):
            for h in range(2):
                t = 2 * k + h
                piece = cube[s * SUB:(s + 1) * SUB, h * BLOCK:(h + 1) * BLOCK] * keeps[s, t]
                a = g1[k, rows(me, s * SUB, SUB), h * BLOCK:(h + 1) * BLOCK].astype(F32)
                up_ref[s * SUB:(s + 1) * SUB, t * BLOCK:(t + 1) * BLOCK] = (
                    lead * a - tail * piece).astype(BF16)

    for g, name, part in ((g1, "a", part1), (g2, "b", part2)):
        sent((name, "out"), g.at[:, 0:7 * ROWS, :])
        sent((name, "sums out", NCH - 1), part.at[NCH - 1])
    sent(("z", "out"), zbuf.at[0:3])
    sent(("t", "out"), tsend.at[0:len(trace_to)])

    @pl.when(direct)
    def _():
        sent(("x", "out"), zbuf.at[:, 0])
        sent(("core", "out"), lhs)

    @pl.when(jnp.logical_not(direct))
    def _():
        sent(("x", "out"), zbuf)


def body(matrix, pattern, shift):
    block = jax.ShapeDtypeStruct((ROWS, COLS), BF16)
    vmem = pl.BlockSpec(memory_space=pltpu.VMEM)
    return pl.pallas_call(
        kernel,
        out_shape=(block, block),
        in_specs=[vmem, pl.BlockSpec(memory_space=pltpu.SMEM), vmem],
        out_specs=(vmem, vmem),
        scratch_shapes=[
            pltpu.VMEM((NCH, DEPTH, CHUNK), BF16),
            pltpu.VMEM((NCH, DEPTH, CHUNK), BF16),
            pltpu.VMEM((4, 2, ROWS, WIDE), BF16),
            pltpu.VMEM((4 * ROWS, DEPTH), BF16),
            pltpu.VMEM((NCH, 3, ROWS, CHUNK), BF16),
            pltpu.VMEM((NCH, 3, ROWS, CHUNK), BF16),
            pltpu.VMEM((NCH, 3, ROWS, CHUNK), BF16),
            pltpu.VMEM((NCH, 3, ROWS, CHUNK), BF16),
            pltpu.VMEM((NCH, ROWS, CHUNK), F32),
            pltpu.VMEM((NCH, ROWS, CHUNK), F32),
            pltpu.VMEM((NCH, 4 * ROWS, CHUNK), F32),
            pltpu.VMEM((9, 8, BLOCK), F32),
            pltpu.VMEM((8, 8, BLOCK), F32),
            pltpu.SemaphoreType.DMA((NSEM,)),
        ],
        compiler_params=pltpu.CompilerParams(
            collective_id=0, has_side_effects=True, vmem_limit_bytes=40 * 2**20),
        cost_estimate=pl.CostEstimate(
            flops=4 * ROWS * COLS * ORDER, bytes_accessed=6 * ROWS * COLS, transcendentals=0),
        name="sign_step",
    )(matrix, pattern, shift.reshape(NBLK, BLOCK))


def solution(mesh):
    placed = (P("col", "row"), P(), P())
    return jax.shard_map(
        body,
        mesh=mesh,
        in_specs=placed,
        out_specs=(P("col", "row"), P("col", "row")),
        check_vma=False,
    )
```

```python
import jax
import jax.numpy as jnp
from jax import lax
from jax.experimental import pallas as pl
from jax.experimental.pallas import tpu as pltpu
from jax.sharding import PartitionSpec as P

BLOCK = 128
ORDER = 6144
NBLK = 48
ROWS = 192
COLS = 768
WIDE = COLS // 2
SUB = 64
CHUNK = 256
NCH = COLS // CHUNK
DEPTH = 8 * ROWS
NQ = 3
PIECE = ROWS // NQ
BAND = 4 * PIECE
NSEM = 81
MESH = pl.DeviceIdType.MESH
F32 = jnp.float32
BF16 = jnp.bfloat16


def kernel(m_hbm, pat_ref, shift_hbm, sq_ref, up_ref,
           m_ref, shift_ref, g1, g2, zbuf, lhs, part1, part2, got1, got2, own1, own2, acc, tsend, trecv, sems):
    r = lax.axis_index("row")
    c = lax.axis_index("col")
    zhi, core = lax.div(r, 2), lax.rem(r, 2)
    y, x, zlo = lax.div(c, 8), lax.rem(lax.div(c, 2), 4), lax.rem(c, 2)
    me = y * 2 + zlo

    ys = {d: lax.rem(y + d, 4) for d in range(1, 4)}
    xs = {d: lax.rem(x + d, 4) for d in range(1, 4)}
    zs = {d: lax.rem(zhi + d, 4) for d in range(1, 4)}
    ys[0], xs[0], zs[0] = y, x, zhi
    y_up, y_down = (r, c + 8 * (ys[1] - y)), (r, c + 8 * (ys[3] - y))
    z_up, z_down = (r + 2 * (zs[1] - zhi), c), (r + 2 * (zs[3] - zhi), c)
    pair_dev = (r, c + 1 - 2 * zlo)
    core_dev = (r + 1 - 2 * core, c)
    x_dev = {d: (r, c + 2 * (xs[d] - x)) for d in range(1, 4)}

    def rows(slot, start=0, size=ROWS):
        return pl.ds(pl.multiple_of(slot * ROWS + start, 16), size)

    loads = [pltpu.make_async_copy(m_hbm, m_ref, sems.at[NSEM]),
             pltpu.make_async_copy(shift_hbm, shift_ref, sems.at[NSEM + 1])]
    for load in loads:
        load.start()

    barrier = pltpu.get_barrier_semaphore()
    partners = [x_dev[1], x_dev[2], x_dev[3], y_up, y_down, z_up, z_down, pair_dev, core_dev]
    for p in partners:
        pl.semaphore_signal(barrier, inc=1, device_id=p, device_id_type=MESH)

    for load in loads:
        load.wait()

    terms = jnp.zeros((SUB, BLOCK), F32)
    keeps = {}
    ahead = (lax.broadcasted_iota(jnp.int32, (SUB, BLOCK), 0)
             - lax.broadcasted_iota(jnp.int32, (SUB, BLOCK), 1))
    for s in range(ROWS // SUB):
        br = lax.div(3 * c + s, 2)
        for t in range(COLS // BLOCK):
            bc = 6 * r + t
            diag = br == bc
            keep = jnp.where((pat_ref[br, bc] > 0) | diag, 1.0, 0.0).astype(F32)
            keep_t = jnp.where((pat_ref[bc, br] > 0) | diag, 1.0, 0.0).astype(F32)
            keeps[s, t] = keep
            m = m_ref[s * SUB:(s + 1) * SUB, t * BLOCK:(t + 1) * BLOCK].astype(F32)
            gap = (r * COLS + t * BLOCK) - (c * ROWS + s * SUB)
            on = jnp.where(ahead == gap, shift_ref[pl.ds(bc, 1), :], 0.0)
            a = (m * keep + on).astype(BF16)
            a_t = (m * keep_t + on).astype(BF16)
            terms += a.astype(F32) * a_t.astype(F32)
            k, lane = t // 2, (t % 2) * BLOCK
            g1[k, rows(me, s * SUB, SUB), lane:lane + BLOCK] = a
            zbuf[zhi, t // 3, s * SUB:(s + 1) * SUB, (t % 3) * BLOCK:(t % 3 + 1) * BLOCK] = a
    tsend[0] = jnp.sum(terms.reshape(SUB // 8, 8, BLOCK), axis=0)

    pl.semaphore_wait(barrier, len(partners))

    index = {}

    def sem(key):
        if key not in index:
            index[key] = len(index)
        return sems.at[index[key]]

    def copy(out, into, src, dst, to):
        return pltpu.make_async_remote_copy(
            src_ref=src, dst_ref=dst, send_sem=sem(out), recv_sem=sem(into),
            device_id=to, device_id_type=MESH)

    def start(out, into, ref, to, dst=None):
        copy(out, into, ref, ref if dst is None else dst, to).start()

    def arrived(key, ref):
        copy(key, key, ref, ref, core_dev).wait_recv()

    def sent(key, ref):
        copy(key, key, ref, ref, core_dev).wait_send()

    slots = {(d, f): rows(ys[d] * 2 + (1 - zlo if f else zlo)) for d in range(4) for f in range(2)}
    tops = {(d, f): rows(ys[d] * 2 + (1 - zlo if f else zlo), 0, ROWS // 2)
            for d in range(4) for f in range(2)}
    ends = {(d, f): rows(ys[d] * 2 + (1 - zlo if f else zlo), ROWS // 2, ROWS // 2)
            for d in range(4) for f in range(2)}

    def own(g, name, k):
        ref = g.at[k, slots[0, 0], :]
        start((name, "out"), (name, "pair", k), ref, pair_dev)
        start((name, "out"), (name, "near", 0, k), ref, y_up)
        start((name, "out"), (name, "near", 0, k), ref, y_down)

    def pair(g, name, k):
        ref = g.at[k, slots[0, 1], :]
        arrived((name, "pair", k), ref)
        start((name, "out"), (name, "near", 1, k), ref, y_up)
        start((name, "out"), (name, "near", 1, k), ref, y_down)

    def near(g, name, k, f):
        arrived((name, "near", f, k), g.at[k, 0:2 * ROWS, :])

    def relay(g, name, k, f):
        near(g, name, k, f)
        start((name, "out"), (name, "far", f, k), g.at[k, tops[3, f], :], y_up)
        start((name, "out"), (name, "far", f, k), g.at[k, ends[1, f], :], y_down)

    def far(g, name, k, f):
        arrived((name, "far", f, k), g.at[k, slots[2, f], :])

    def far_pair(g, name, k):
        far(g, name, k, 0)
        start((name, "out"), (name, "far", 1, k), g.at[k, slots[2, 0], :], pair_dev)

    def along_z(q):
        ref = zbuf.at[zhi, :, q * PIECE:(q + 1) * PIECE, :]
        start(("z", "out"), ("z", q), ref, z_up)
        start(("z", "out"), ("z", q), ref, z_down)

    direct = core == lax.div(x, 2)
    depth = {d: pl.ds(pl.multiple_of(zs[d] * WIDE, BLOCK), WIDE) for d in range(4)}
    to_x = [core * 2 + h for h in range(2)]
    home = lax.rem(x, 2)

    def along_x(d, q):
        into = pl.ds(pl.multiple_of(q * BAND + x * PIECE, 16), PIECE)
        dst = lhs.at[into, depth[d]]
        for h in range(2):
            src = zbuf.at[zs[d], h, q * PIECE:(q + 1) * PIECE, :]

            @pl.when(to_x[h] != x)
            def _(h=h, src=src):
                start(("x", "out"), ("x", d, q), src, (r, c + 2 * (to_x[h] - x)), dst)

            @pl.when(to_x[h] == x)
            def _(h=h):
                lhs[into, depth[d]] = zbuf[zs[d], h, q * PIECE:(q + 1) * PIECE, :]

    def relay_z(q):
        arrived(("z", q), zbuf.at[0:2, :, 0:PIECE, :])
        half = PIECE // 2
        for back, row, first in ((3, z_up[0], 0), (1, z_down[0], half)):
            into = pl.ds(pl.multiple_of(q * BAND + x * PIECE + first, 16), half)
            low = q * PIECE + first
            for h in range(2):
                start(("z", "out"), ("x", 2, q), zbuf.at[zs[back], h, low:low + half, :],
                      (row, c + 2 * (to_x[h] - x)), lhs.at[into, depth[back]])

    def to_core(d, q):
        ref = lhs.at[q * BAND:(q + 1) * BAND, depth[d]]

        @pl.when(direct)
        def _():
            arrived(("x", d, q), lhs.at[0:(4 if d == 2 else 3) * PIECE, depth[d]])
            start(("core", "out"), ("core", d, q), ref, core_dev)

    def from_core(d, q):
        @pl.when(jnp.logical_not(direct))
        def _():
            arrived(("core", d, q), lhs.at[q * BAND:(q + 1) * BAND, depth[d]])

    odd_x, odd_z, odd_y = lax.rem(x, 2), lax.rem(zhi, 2), lax.rem(y, 2)

    def step(first, d1, d3):
        return tuple(jnp.where(first, u, v) for u, v in zip(d1, d3))

    trace_to = [
        core_dev, pair_dev,
        step(odd_x == 0, x_dev[1], x_dev[3]), step(odd_x == 1, x_dev[1], x_dev[3]),
        step(odd_y == 0, y_up, y_down), step(odd_y == 1, y_up, y_down),
        step(odd_z == 0, z_up, z_down), step(odd_z == 1, z_up, z_down),
    ]

    def trace_send(i):
        start(("t", "out"), ("t", i), tsend.at[i], trace_to[i], trecv.at[i])

    def trace_sum(i):
        arrived(("t", i), trecv.at[i])
        tsend[i + 1] = tsend[i] + trecv[i]
        if i + 1 < len(trace_to):
            trace_send(i + 1)

    def span(slot):
        return pl.ds(pl.multiple_of(slot * WIDE, BLOCK), WIDE)

    def part_dot(g, k, slot, first=False, band=None):
        band = pl.ds(0, 4 * ROWS) if band is None else band
        term = jnp.dot(lhs[band, span(slot)], g[k, span(slot), :], preferred_element_type=F32)
        acc[k, band] = term if first else acc[k, band] + term

    def piece(k, q, d):
        return acc[k, pl.ds(pl.multiple_of(q * BAND + xs[d] * PIECE, 16), PIECE), :]

    def ship_band(k, q):
        band = pl.ds(q * PIECE, PIECE)
        for d in (2, 1, 3):
            part1[k, d - 1, band] = piece(k, q, d).astype(BF16)
            start(("a", "sums out"), ("a", "sums", k), part1.at[k, d - 1, band, :], x_dev[d],
                  got1.at[k, d - 1, band, :])
        own1[k, band] = piece(k, q, 0)

    def early(q):
        band = pl.ds(q * BAND, BAND)
        for k in range(NCH):
            acc[k, band] = jnp.dot(lhs[band, :], g1[k], preferred_element_type=F32)
            ship_band(k, q)

    def ship(k):
        for d in (2, 1, 3):
            for q in range(NQ):
                part2[k, d - 1, q * PIECE:(q + 1) * PIECE] = piece(k, q, d).astype(BF16)
        if k:
            sent(("b", "sums out", k - 1), part2.at[k - 1])
        for d in (2, 1, 3):
            start(("b", "sums out", k), ("b", "sums", k), part2.at[k, d - 1], x_dev[d],
                  got2.at[k, d - 1])
        for q in range(NQ):
            own2[k, q * PIECE:(q + 1) * PIECE] = piece(k, q, 0)

    def total(got, kept, name, k):
        arrived((name, "sums", k), got.at[k])
        return kept[k] + (got[k, 0].astype(F32) + got[k, 2].astype(F32)) + got[k, 1].astype(F32)

    own(g1, "a", 0)
    own(g1, "a", 1)
    own(g1, "a", 2)
    along_z(0)
    along_z(1)
    along_z(2)
    along_x(0, 0)
    along_x(0, 1)
    along_x(0, 2)
    trace_send(0)
    pair(g1, "a", 0)
    relay(g1, "a", 0, 0)
    pair(g1, "a", 1)
    relay(g1, "a", 1, 0)
    relay_z(0)
    along_x(3, 0)
    along_x(1, 0)
    pair(g1, "a", 2)
    relay(g1, "a", 2, 0)
    relay_z(1)
    along_x(3, 1)
    along_x(1, 1)
    trace_sum(0)
    relay(g1, "a", 0, 1)
    relay_z(2)
    along_x(3, 2)
    along_x(1, 2)
    for d in (0, 3, 1):
        to_core(d, 0)
    relay(g1, "a", 1, 1)
    to_core(2, 0)
    relay(g1, "a", 2, 1)
    trace_sum(1)
    for k in range(NCH):
        far(g1, "a", k, 0)
        far(g1, "a", k, 1)
    for d in (0, 3, 1):
        from_core(d, 0)
    from_core(2, 0)
    for d in (0, 3, 1):
        to_core(d, 1)
    early(0)
    to_core(2, 1)
    for d in (0, 3, 1):
        to_core(d, 2)
    for d in (0, 3, 1):
        from_core(d, 1)
    from_core(2, 1)
    early(1)
    for d in (0, 3, 1):
        from_core(d, 2)
    for k in range(NCH):
        for d in (0, 3, 1):
            part_dot(g1, k, zs[d], d == 0, pl.ds(2 * BAND, BAND))
    to_core(2, 2)
    from_core(2, 2)
    for k in range(NCH):
        part_dot(g1, k, zs[2], band=pl.ds(2 * BAND, BAND))
        ship_band(k, 2)
    def squares(k):
        full = total(got1, own1, "a", k)
        for s in range(ROWS // SUB):
            for h in range(2):
                t = 2 * k + h
                piece = full[s * SUB:(s + 1) * SUB, h * BLOCK:(h + 1) * BLOCK] * keeps[s, t]
                piece = piece.astype(BF16)
                g2[k, rows(me, s * SUB, SUB), h * BLOCK:(h + 1) * BLOCK] = piece
                sq_ref[s * SUB:(s + 1) * SUB, t * BLOCK:(t + 1) * BLOCK] = piece
        own(g2, "b", k)

    squares(0)
    trace_sum(2)
    pair(g2, "b", 0)
    relay(g2, "b", 0, 0)
    squares(1)
    trace_sum(3)
    far_pair(g2, "b", 0)
    pair(g2, "b", 1)
    relay(g2, "b", 1, 0)
    part_dot(g2, 0, ys[0], True)
    squares(2)
    trace_sum(4)
    near(g2, "b", 0, 1)
    part_dot(g2, 0, ys[1])
    part_dot(g2, 0, ys[3])
    far_pair(g2, "b", 1)
    part_dot(g2, 1, ys[0], True)
    pair(g2, "b", 2)
    relay(g2, "b", 2, 0)
    far(g2, "b", 0, 1)
    part_dot(g2, 0, ys[2])
    ship(0)
    near(g2, "b", 1, 1)
    part_dot(g2, 1, ys[1])
    part_dot(g2, 1, ys[3])
    far_pair(g2, "b", 2)
    part_dot(g2, 2, ys[0], True)
    far(g2, "b", 1, 1)
    part_dot(g2, 1, ys[2])
    trace_sum(5)
    ship(1)
    near(g2, "b", 2, 1)
    part_dot(g2, 2, ys[1])
    part_dot(g2, 2, ys[3])
    trace_sum(6)
    far(g2, "b", 2, 1)
    part_dot(g2, 2, ys[2])
    ship(2)
    trace_sum(7)

    trace = jnp.sum(tsend[len(trace_to)], keepdims=True)
    gamma = jnp.sqrt(ORDER / jnp.maximum(jnp.abs(trace), 1.0))
    lead, tail = 1.5 * gamma, 0.5 * gamma * gamma * gamma
    for k in range(NCH):
        cube = total(got2, own2, "b", k)
        for s in range(ROWS // SUB):
            for h in range(2):
                t = 2 * k + h
                piece = cube[s * SUB:(s + 1) * SUB, h * BLOCK:(h + 1) * BLOCK] * keeps[s, t]
                a = g1[k, rows(me, s * SUB, SUB), h * BLOCK:(h + 1) * BLOCK].astype(F32)
                up_ref[s * SUB:(s + 1) * SUB, t * BLOCK:(t + 1) * BLOCK] = (
                    lead * a - tail * piece).astype(BF16)

    sent(("a", "out"), g1.at[:, 0:7 * ROWS, :])
    sent(("b", "out"), g2.at[:, 0:7 * ROWS, :])
    sent(("a", "sums out"), part1)
    sent(("b", "sums out", NCH - 1), part2.at[NCH - 1])
    sent(("z", "out"), zbuf.at[0:3])
    sent(("t", "out"), tsend.at[0:len(trace_to)])

    @pl.when(direct)
    def _():
        sent(("x", "out"), zbuf.at[0:3, 0])
        sent(("core", "out"), lhs)

    @pl.when(jnp.logical_not(direct))
    def _():
        sent(("x", "out"), zbuf.at[0:3])


def publish(sq_ref, up_ref, sq_out, up_out, sems):
    copies = [pltpu.make_async_copy(sq_ref, sq_out, sems.at[0]),
              pltpu.make_async_copy(up_ref, up_out, sems.at[1])]
    for copy in copies:
        copy.start()
    for copy in copies:
        copy.wait()


def body(matrix, pattern, shift):
    block = jax.ShapeDtypeStruct((ROWS, COLS), BF16)
    vmem = pl.BlockSpec(memory_space=pltpu.VMEM)
    hbm = pl.BlockSpec(memory_space=pltpu.HBM)
    results = pl.pallas_call(
        kernel,
        out_shape=(block, block),
        in_specs=[hbm, pl.BlockSpec(memory_space=pltpu.SMEM), hbm],
        out_specs=(vmem, vmem),
        scratch_shapes=[
            pltpu.VMEM((ROWS, COLS), BF16),
            pltpu.VMEM((NBLK, BLOCK), F32),
            pltpu.VMEM((NCH, DEPTH, CHUNK), BF16),
            pltpu.VMEM((NCH, DEPTH, CHUNK), BF16),
            pltpu.VMEM((4, 2, ROWS, WIDE), BF16),
            pltpu.VMEM((4 * ROWS, DEPTH), BF16),
            pltpu.VMEM((NCH, 3, ROWS, CHUNK), BF16),
            pltpu.VMEM((NCH, 3, ROWS, CHUNK), BF16),
            pltpu.VMEM((NCH, 3, ROWS, CHUNK), BF16),
            pltpu.VMEM((NCH, 3, ROWS, CHUNK), BF16),
            pltpu.VMEM((NCH, ROWS, CHUNK), F32),
            pltpu.VMEM((NCH, ROWS, CHUNK), F32),
            pltpu.VMEM((NCH, 4 * ROWS, CHUNK), F32),
            pltpu.VMEM((9, 8, BLOCK), F32),
            pltpu.VMEM((8, 8, BLOCK), F32),
            pltpu.SemaphoreType.DMA((NSEM + 2,)),
        ],
        compiler_params=pltpu.CompilerParams(
            collective_id=0, has_side_effects=True, vmem_limit_bytes=60 * 2**20),
        cost_estimate=pl.CostEstimate(
            flops=4 * ROWS * COLS * ORDER, bytes_accessed=6 * ROWS * COLS, transcendentals=0),
        name="sign_step",
    )(matrix, pattern, shift.reshape(NBLK, BLOCK))
    return pl.pallas_call(
        publish,
        out_shape=(block, block),
        in_specs=[vmem, vmem],
        out_specs=(hbm, hbm),
        scratch_shapes=[pltpu.SemaphoreType.DMA((2,))],
        name="publish",
    )(*results)


def solution(mesh):
    placed = (P("col", "row"), P(), P())
    return jax.shard_map(
        body,
        mesh=mesh,
        in_specs=placed,
        out_specs=(P("col", "row"), P("col", "row")),
        check_vma=False,
    )
```

```python
import jax
import jax.numpy as jnp
from jax import lax
from jax.experimental import pallas as pl
from jax.experimental.pallas import tpu as pltpu
from jax.sharding import PartitionSpec as P

BLOCK = 128
ORDER = 6144
NBLK = 48
ROWS = 192
COLS = 768
WIDE = COLS // 2
SUB = 64
CHUNK = 256
NCH = COLS // CHUNK
DEPTH = 8 * ROWS
NQ = 3
PIECE = ROWS // NQ
BAND = 4 * PIECE
NSEM = 81
MESH = pl.DeviceIdType.MESH
F32 = jnp.float32
BF16 = jnp.bfloat16


def kernel(m_hbm, pat_ref, shift_hbm, sq_ref, up_ref,
           m_ref, shift_ref, g1, g2, zbuf, lhs, part1, part2, got1, got2, own1, own2, acc, tsend, trecv, sems):
    r = lax.axis_index("row")
    c = lax.axis_index("col")
    zhi, core = lax.div(r, 2), lax.rem(r, 2)
    y, x, zlo = lax.div(c, 8), lax.rem(lax.div(c, 2), 4), lax.rem(c, 2)
    me = y * 2 + zlo

    ys = {d: lax.rem(y + d, 4) for d in range(1, 4)}
    xs = {d: lax.rem(x + d, 4) for d in range(1, 4)}
    zs = {d: lax.rem(zhi + d, 4) for d in range(1, 4)}
    ys[0], xs[0], zs[0] = y, x, zhi
    y_up, y_down = (r, c + 8 * (ys[1] - y)), (r, c + 8 * (ys[3] - y))
    z_up, z_down = (r + 2 * (zs[1] - zhi), c), (r + 2 * (zs[3] - zhi), c)
    pair_dev = (r, c + 1 - 2 * zlo)
    core_dev = (r + 1 - 2 * core, c)
    x_dev = {d: (r, c + 2 * (xs[d] - x)) for d in range(1, 4)}

    def rows(slot, start=0, size=ROWS):
        return pl.ds(pl.multiple_of(slot * ROWS + start, 16), size)

    loads = [pltpu.make_async_copy(m_hbm, m_ref, sems.at[NSEM]),
             pltpu.make_async_copy(shift_hbm, shift_ref, sems.at[NSEM + 1])]
    for load in loads:
        load.start()

    barrier = pltpu.get_barrier_semaphore()
    partners = [x_dev[1], x_dev[2], x_dev[3], y_up, y_down, z_up, z_down, pair_dev, core_dev]
    for p in partners:
        pl.semaphore_signal(barrier, inc=1, device_id=p, device_id_type=MESH)

    for load in loads:
        load.wait()

    terms = jnp.zeros((SUB, BLOCK), F32)
    keeps = {}
    ahead = (lax.broadcasted_iota(jnp.int32, (SUB, BLOCK), 0)
             - lax.broadcasted_iota(jnp.int32, (SUB, BLOCK), 1))
    for s in range(ROWS // SUB):
        br = lax.div(3 * c + s, 2)
        for t in range(COLS // BLOCK):
            bc = 6 * r + t
            diag = br == bc
            keep = jnp.where((pat_ref[br, bc] > 0) | diag, 1.0, 0.0).astype(F32)
            keep_t = jnp.where((pat_ref[bc, br] > 0) | diag, 1.0, 0.0).astype(F32)
            keeps[s, t] = keep
            m = m_ref[s * SUB:(s + 1) * SUB, t * BLOCK:(t + 1) * BLOCK].astype(F32)
            gap = (r * COLS + t * BLOCK) - (c * ROWS + s * SUB)
            on = jnp.where(ahead == gap, shift_ref[pl.ds(bc, 1), :], 0.0)
            a = (m * keep + on).astype(BF16)
            a_t = (m * keep_t + on).astype(BF16)
            terms += a.astype(F32) * a_t.astype(F32)
            k, lane = t // 2, (t % 2) * BLOCK
            g1[k, rows(me, s * SUB, SUB), lane:lane + BLOCK] = a
            zbuf[zhi, t // 3, s * SUB:(s + 1) * SUB, (t % 3) * BLOCK:(t % 3 + 1) * BLOCK] = a
    tsend[0] = jnp.sum(terms.reshape(SUB // 8, 8, BLOCK), axis=0)

    pl.semaphore_wait(barrier, len(partners))

    index = {}

    def sem(key):
        if key not in index:
            index[key] = len(index)
        return sems.at[index[key]]

    def copy(out, into, src, dst, to):
        return pltpu.make_async_remote_copy(
            src_ref=src, dst_ref=dst, send_sem=sem(out), recv_sem=sem(into),
            device_id=to, device_id_type=MESH)

    def start(out, into, ref, to, dst=None):
        copy(out, into, ref, ref if dst is None else dst, to).start()

    def arrived(key, ref):
        copy(key, key, ref, ref, core_dev).wait_recv()

    def sent(key, ref):
        copy(key, key, ref, ref, core_dev).wait_send()

    slots = {(d, f): rows(ys[d] * 2 + (1 - zlo if f else zlo)) for d in range(4) for f in range(2)}
    tops = {(d, f): rows(ys[d] * 2 + (1 - zlo if f else zlo), 0, ROWS // 2)
            for d in range(4) for f in range(2)}
    ends = {(d, f): rows(ys[d] * 2 + (1 - zlo if f else zlo), ROWS // 2, ROWS // 2)
            for d in range(4) for f in range(2)}

    def own(g, name, k):
        ref = g.at[k, slots[0, 0], :]
        start((name, "out"), (name, "pair", k), ref, pair_dev)
        start((name, "out"), (name, "near", 0, k), ref, y_up)
        start((name, "out"), (name, "near", 0, k), ref, y_down)

    def pair(g, name, k):
        ref = g.at[k, slots[0, 1], :]
        arrived((name, "pair", k), ref)
        start((name, "out"), (name, "near", 1, k), ref, y_up)
        start((name, "out"), (name, "near", 1, k), ref, y_down)

    def near(g, name, k, f):
        arrived((name, "near", f, k), g.at[k, 0:2 * ROWS, :])

    def relay(g, name, k, f):
        near(g, name, k, f)
        start((name, "out"), (name, "far", f, k), g.at[k, tops[3, f], :], y_up)
        start((name, "out"), (name, "far", f, k), g.at[k, ends[1, f], :], y_down)

    def far(g, name, k, f):
        arrived((name, "far", f, k), g.at[k, slots[2, f], :])

    def far_pair(g, name, k):
        far(g, name, k, 0)
        start((name, "out"), (name, "far", 1, k), g.at[k, slots[2, 0], :], pair_dev)

    def along_z(q):
        ref = zbuf.at[zhi, :, q * PIECE:(q + 1) * PIECE, :]
        start(("z", "out"), ("z", q), ref, z_up)
        start(("z", "out"), ("z", q), ref, z_down)

    direct = core == lax.div(x, 2)
    depth = {d: pl.ds(pl.multiple_of(zs[d] * WIDE, BLOCK), WIDE) for d in range(4)}
    to_x = [core * 2 + h for h in range(2)]
    home = lax.rem(x, 2)

    def along_x(d, q):
        into = pl.ds(pl.multiple_of(q * BAND + x * PIECE, 16), PIECE)
        dst = lhs.at[into, depth[d]]
        for h in range(2):
            src = zbuf.at[zs[d], h, q * PIECE:(q + 1) * PIECE, :]

            @pl.when(to_x[h] != x)
            def _(h=h, src=src):
                start(("x", "out"), ("x", d, q), src, (r, c + 2 * (to_x[h] - x)), dst)

            @pl.when(to_x[h] == x)
            def _(h=h):
                lhs[into, depth[d]] = zbuf[zs[d], h, q * PIECE:(q + 1) * PIECE, :]

    def relay_z(q):
        arrived(("z", q), zbuf.at[0:2, :, 0:PIECE, :])
        half = PIECE // 2
        for back, row, first in ((3, z_up[0], 0), (1, z_down[0], half)):
            into = pl.ds(pl.multiple_of(q * BAND + x * PIECE + first, 16), half)
            low = q * PIECE + first
            for h in range(2):
                start(("z", "out"), ("x", 2, q), zbuf.at[zs[back], h, low:low + half, :],
                      (row, c + 2 * (to_x[h] - x)), lhs.at[into, depth[back]])

    def to_core(d, q):
        ref = lhs.at[q * BAND:(q + 1) * BAND, depth[d]]

        @pl.when(direct)
        def _():
            arrived(("x", d, q), lhs.at[0:(4 if d == 2 else 3) * PIECE, depth[d]])
            start(("core", "out"), ("core", d, q), ref, core_dev)

    def from_core(d, q):
        @pl.when(jnp.logical_not(direct))
        def _():
            arrived(("core", d, q), lhs.at[q * BAND:(q + 1) * BAND, depth[d]])

    odd_x, odd_z, odd_y = lax.rem(x, 2), lax.rem(zhi, 2), lax.rem(y, 2)

    def step(first, d1, d3):
        return tuple(jnp.where(first, u, v) for u, v in zip(d1, d3))

    trace_to = [
        core_dev, pair_dev,
        step(odd_x == 0, x_dev[1], x_dev[3]), step(odd_x == 1, x_dev[1], x_dev[3]),
        step(odd_y == 0, y_up, y_down), step(odd_y == 1, y_up, y_down),
        step(odd_z == 0, z_up, z_down), step(odd_z == 1, z_up, z_down),
    ]

    def trace_send(i):
        start(("t", "out"), ("t", i), tsend.at[i], trace_to[i], trecv.at[i])

    def trace_sum(i):
        arrived(("t", i), trecv.at[i])
        tsend[i + 1] = tsend[i] + trecv[i]
        if i + 1 < len(trace_to):
            trace_send(i + 1)

    def span(slot):
        return pl.ds(pl.multiple_of(slot * WIDE, BLOCK), WIDE)

    def part_dot(g, k, slot, first=False, band=None):
        band = pl.ds(0, 4 * ROWS) if band is None else band
        term = jnp.dot(lhs[band, span(slot)], g[k, span(slot), :], preferred_element_type=F32)
        acc[k, band] = term if first else acc[k, band] + term

    def piece(k, q, d):
        return acc[k, pl.ds(pl.multiple_of(q * BAND + xs[d] * PIECE, 16), PIECE), :]

    def ship_band(k, q):
        band = pl.ds(q * PIECE, PIECE)
        for d in (2, 1, 3):
            part1[k, d - 1, band] = piece(k, q, d).astype(BF16)
            start(("a", "sums out"), ("a", "sums", k), part1.at[k, d - 1, band, :], x_dev[d],
                  got1.at[k, d - 1, band, :])
        own1[k, band] = piece(k, q, 0)

    def early(q, k):
        band = pl.ds(q * BAND, BAND)
        acc[k, band] = jnp.dot(lhs[band, :], g1[k], preferred_element_type=F32)
        ship_band(k, q)

    def ship(k):
        for d in (2, 1, 3):
            for q in range(NQ):
                part2[k, d - 1, q * PIECE:(q + 1) * PIECE] = piece(k, q, d).astype(BF16)
        for d in (2, 1, 3):
            start(("b", "sums out"), ("b", "sums", k), part2.at[k, d - 1], x_dev[d],
                  got2.at[k, d - 1])
        for q in range(NQ):
            own2[k, q * PIECE:(q + 1) * PIECE] = piece(k, q, 0)

    def total(got, kept, name, k):
        arrived((name, "sums", k), got.at[k])
        return kept[k] + (got[k, 0].astype(F32) + got[k, 2].astype(F32)) + got[k, 1].astype(F32)

    own(g1, "a", 0)
    own(g1, "a", 1)
    own(g1, "a", 2)
    along_z(0)
    along_z(1)
    along_z(2)
    along_x(0, 0)
    along_x(0, 1)
    along_x(0, 2)
    trace_send(0)
    pair(g1, "a", 0)
    relay(g1, "a", 0, 0)
    pair(g1, "a", 1)
    relay(g1, "a", 1, 0)
    pair(g1, "a", 2)
    relay(g1, "a", 2, 0)
    relay_z(0)
    along_x(3, 0)
    along_x(1, 0)
    relay(g1, "a", 0, 1)
    relay_z(1)
    along_x(3, 1)
    along_x(1, 1)
    relay(g1, "a", 1, 1)
    relay(g1, "a", 2, 1)
    relay_z(2)
    along_x(3, 2)
    along_x(1, 2)
    for d in (0, 3, 1):
        to_core(d, 0)
    to_core(2, 0)
    far(g1, "a", 0, 0)
    far(g1, "a", 0, 1)
    far(g1, "a", 1, 0)
    far(g1, "a", 1, 1)
    far(g1, "a", 2, 0)
    far(g1, "a", 2, 1)
    for d in (0, 3, 1):
        from_core(d, 0)
    from_core(2, 0)
    for k in range(NCH):
        early(0, k)
    for d in (0, 3, 1):
        to_core(d, 1)
    to_core(2, 1)
    for d in (0, 3, 1):
        from_core(d, 1)
    from_core(2, 1)
    early(1, 0)
    early(1, 1)
    early(1, 2)
    trace_sum(0)
    for d in (0, 3, 1):
        to_core(d, 2)
    for d in (0, 3, 1):
        from_core(d, 2)
    for k in range(NCH):
        for d in (0, 3, 1):
            part_dot(g1, k, zs[d], d == 0, pl.ds(2 * BAND, BAND))
    to_core(2, 2)
    from_core(2, 2)
    for k in range(NCH):
        part_dot(g1, k, zs[2], band=pl.ds(2 * BAND, BAND))
        ship_band(k, 2)
    trace_sum(1)
    def squares(k):
        full = total(got1, own1, "a", k)
        for s in range(ROWS // SUB):
            for h in range(2):
                t = 2 * k + h
                piece = full[s * SUB:(s + 1) * SUB, h * BLOCK:(h + 1) * BLOCK] * keeps[s, t]
                piece = piece.astype(BF16)
                g2[k, rows(me, s * SUB, SUB), h * BLOCK:(h + 1) * BLOCK] = piece
                sq_ref[s * SUB:(s + 1) * SUB, t * BLOCK:(t + 1) * BLOCK] = piece
        own(g2, "b", k)

    squares(0)
    squares(1)
    trace_sum(2)
    pair(g2, "b", 0)
    relay(g2, "b", 0, 0)
    squares(2)
    part_dot(g2, 0, ys[0], True)
    pair(g2, "b", 1)
    relay(g2, "b", 1, 0)
    far_pair(g2, "b", 0)
    trace_sum(3)
    part_dot(g2, 1, ys[0], True)
    pair(g2, "b", 2)
    relay(g2, "b", 2, 0)
    near(g2, "b", 0, 1)
    part_dot(g2, 0, ys[1])
    part_dot(g2, 0, ys[3])
    far_pair(g2, "b", 1)
    trace_sum(4)
    part_dot(g2, 2, ys[0], True)
    far(g2, "b", 0, 1)
    part_dot(g2, 0, ys[2])
    ship(0)
    near(g2, "b", 1, 1)
    part_dot(g2, 1, ys[1])
    part_dot(g2, 1, ys[3])
    far_pair(g2, "b", 2)
    trace_sum(5)
    far(g2, "b", 1, 1)
    part_dot(g2, 1, ys[2])
    ship(1)
    near(g2, "b", 2, 1)
    part_dot(g2, 2, ys[1])
    part_dot(g2, 2, ys[3])
    trace_sum(6)
    far(g2, "b", 2, 1)
    part_dot(g2, 2, ys[2])
    ship(2)
    trace_sum(7)

    trace = jnp.sum(tsend[len(trace_to)], keepdims=True)
    gamma = jnp.sqrt(ORDER / jnp.maximum(jnp.abs(trace), 1.0))
    lead, tail = 1.5 * gamma, 0.5 * gamma * gamma * gamma
    for k in range(NCH):
        cube = total(got2, own2, "b", k)
        for s in range(ROWS // SUB):
            for h in range(2):
                t = 2 * k + h
                piece = cube[s * SUB:(s + 1) * SUB, h * BLOCK:(h + 1) * BLOCK] * keeps[s, t]
                a = g1[k, rows(me, s * SUB, SUB), h * BLOCK:(h + 1) * BLOCK].astype(F32)
                up_ref[s * SUB:(s + 1) * SUB, t * BLOCK:(t + 1) * BLOCK] = (
                    lead * a - tail * piece).astype(BF16)

    sent(("a", "out"), g1.at[:, 0:7 * ROWS, :])
    sent(("b", "out"), g2.at[:, 0:7 * ROWS, :])
    sent(("a", "sums out"), part1)
    sent(("b", "sums out"), part2)
    sent(("z", "out"), zbuf.at[0:3])
    sent(("t", "out"), tsend.at[0:len(trace_to)])

    @pl.when(direct)
    def _():
        sent(("x", "out"), zbuf.at[0:3, 0])
        sent(("core", "out"), lhs)

    @pl.when(jnp.logical_not(direct))
    def _():
        sent(("x", "out"), zbuf.at[0:3])


def publish(sq_ref, up_ref, sq_out, up_out, sems):
    copies = [pltpu.make_async_copy(sq_ref, sq_out, sems.at[0]),
              pltpu.make_async_copy(up_ref, up_out, sems.at[1])]
    for copy in copies:
        copy.start()
    for copy in copies:
        copy.wait()


def body(matrix, pattern, shift):
    block = jax.ShapeDtypeStruct((ROWS, COLS), BF16)
    vmem = pl.BlockSpec(memory_space=pltpu.VMEM)
    hbm = pl.BlockSpec(memory_space=pltpu.HBM)
    results = pl.pallas_call(
        kernel,
        out_shape=(block, block),
        in_specs=[hbm, pl.BlockSpec(memory_space=pltpu.SMEM), hbm],
        out_specs=(vmem, vmem),
        scratch_shapes=[
            pltpu.VMEM((ROWS, COLS), BF16),
            pltpu.VMEM((NBLK, BLOCK), F32),
            pltpu.VMEM((NCH, DEPTH, CHUNK), BF16),
            pltpu.VMEM((NCH, DEPTH, CHUNK), BF16),
            pltpu.VMEM((4, 2, ROWS, WIDE), BF16),
            pltpu.VMEM((4 * ROWS, DEPTH), BF16),
            pltpu.VMEM((NCH, 3, ROWS, CHUNK), BF16),
            pltpu.VMEM((NCH, 3, ROWS, CHUNK), BF16),
            pltpu.VMEM((NCH, 3, ROWS, CHUNK), BF16),
            pltpu.VMEM((NCH, 3, ROWS, CHUNK), BF16),
            pltpu.VMEM((NCH, ROWS, CHUNK), F32),
            pltpu.VMEM((NCH, ROWS, CHUNK), F32),
            pltpu.VMEM((NCH, 4 * ROWS, CHUNK), F32),
            pltpu.VMEM((9, 8, BLOCK), F32),
            pltpu.VMEM((8, 8, BLOCK), F32),
            pltpu.SemaphoreType.DMA((NSEM + 2,)),
        ],
        compiler_params=pltpu.CompilerParams(
            collective_id=0, has_side_effects=True, vmem_limit_bytes=60 * 2**20),
        cost_estimate=pl.CostEstimate(
            flops=4 * ROWS * COLS * ORDER, bytes_accessed=6 * ROWS * COLS, transcendentals=0),
        name="sign_step",
    )(matrix, pattern, shift.reshape(NBLK, BLOCK))
    return pl.pallas_call(
        publish,
        out_shape=(block, block),
        in_specs=[vmem, vmem],
        out_specs=(hbm, hbm),
        scratch_shapes=[pltpu.SemaphoreType.DMA((2,))],
        name="publish",
    )(*results)


def solution(mesh):
    placed = (P("col", "row"), P(), P())
    return jax.shard_map(
        body,
        mesh=mesh,
        in_specs=placed,
        out_specs=(P("col", "row"), P("col", "row")),
        check_vma=False,
    )
```

```python
import jax
import jax.numpy as jnp
from jax import lax
from jax.experimental import pallas as pl
from jax.experimental.pallas import tpu as pltpu
from jax.sharding import PartitionSpec as P

BLOCK = 128
ORDER = 6144
NBLK = 48
ROWS = 192
COLS = 768
WIDE = COLS // 2
SUB = 64
CHUNK = 256
NCH = COLS // CHUNK
DEPTH = 8 * ROWS
NQ = 3
PIECE = ROWS // NQ
BAND = 4 * PIECE
NSEM = 81
MESH = pl.DeviceIdType.MESH
F32 = jnp.float32
BF16 = jnp.bfloat16


def kernel(m_hbm, pat_ref, shift_hbm, sq_ref, up_ref,
           m_ref, shift_ref, g1, g2, zbuf, lhs, part1, part2, got1, got2, own1, own2, acc, tsend, trecv, sems):
    r = lax.axis_index("row")
    c = lax.axis_index("col")
    zhi, core = lax.div(r, 2), lax.rem(r, 2)
    y, x, zlo = lax.div(c, 8), lax.rem(lax.div(c, 2), 4), lax.rem(c, 2)
    me = y * 2 + zlo

    ys = {d: lax.rem(y + d, 4) for d in range(1, 4)}
    xs = {d: lax.rem(x + d, 4) for d in range(1, 4)}
    zs = {d: lax.rem(zhi + d, 4) for d in range(1, 4)}
    ys[0], xs[0], zs[0] = y, x, zhi
    y_up, y_down = (r, c + 8 * (ys[1] - y)), (r, c + 8 * (ys[3] - y))
    z_up, z_down = (r + 2 * (zs[1] - zhi), c), (r + 2 * (zs[3] - zhi), c)
    pair_dev = (r, c + 1 - 2 * zlo)
    core_dev = (r + 1 - 2 * core, c)
    x_dev = {d: (r, c + 2 * (xs[d] - x)) for d in range(1, 4)}

    def rows(slot, start=0, size=ROWS):
        return pl.ds(pl.multiple_of(slot * ROWS + start, 16), size)

    loads = [pltpu.make_async_copy(m_hbm, m_ref, sems.at[NSEM]),
             pltpu.make_async_copy(shift_hbm, shift_ref, sems.at[NSEM + 1])]
    for load in loads:
        load.start()

    barrier = pltpu.get_barrier_semaphore()
    partners = [x_dev[1], x_dev[2], x_dev[3], y_up, y_down, z_up, z_down, pair_dev, core_dev]
    for p in partners:
        pl.semaphore_signal(barrier, inc=1, device_id=p, device_id_type=MESH)

    for load in loads:
        load.wait()

    terms = jnp.zeros((SUB, BLOCK), F32)
    keeps = {}
    ahead = (lax.broadcasted_iota(jnp.int32, (SUB, BLOCK), 0)
             - lax.broadcasted_iota(jnp.int32, (SUB, BLOCK), 1))
    def build(part, sums):
        for s in range(ROWS // SUB):
            br = lax.div(3 * c + s, 2)
            for t in (2 * part, 2 * part + 1):
                bc = 6 * r + t
                diag = br == bc
                keep = jnp.where((pat_ref[br, bc] > 0) | diag, 1.0, 0.0).astype(F32)
                keep_t = jnp.where((pat_ref[bc, br] > 0) | diag, 1.0, 0.0).astype(F32)
                keeps[s, t] = keep
                m = m_ref[s * SUB:(s + 1) * SUB, t * BLOCK:(t + 1) * BLOCK].astype(F32)
                gap = (r * COLS + t * BLOCK) - (c * ROWS + s * SUB)
                on = jnp.where(ahead == gap, shift_ref[pl.ds(bc, 1), :], 0.0)
                a = (m * keep + on).astype(BF16)
                a_t = (m * keep_t + on).astype(BF16)
                sums += a.astype(F32) * a_t.astype(F32)
                k, lane = t // 2, (t % 2) * BLOCK
                g1[k, rows(me, s * SUB, SUB), lane:lane + BLOCK] = a
                zbuf[zhi, t // 3, s * SUB:(s + 1) * SUB, (t % 3) * BLOCK:(t % 3 + 1) * BLOCK] = a
        return sums

    terms = build(0, terms)
    pl.semaphore_wait(barrier, len(partners))

    index = {}

    def sem(key):
        if key not in index:
            index[key] = len(index)
        return sems.at[index[key]]

    def copy(out, into, src, dst, to):
        return pltpu.make_async_remote_copy(
            src_ref=src, dst_ref=dst, send_sem=sem(out), recv_sem=sem(into),
            device_id=to, device_id_type=MESH)

    def start(out, into, ref, to, dst=None):
        copy(out, into, ref, ref if dst is None else dst, to).start()

    def arrived(key, ref):
        copy(key, key, ref, ref, core_dev).wait_recv()

    def sent(key, ref):
        copy(key, key, ref, ref, core_dev).wait_send()

    slots = {(d, f): rows(ys[d] * 2 + (1 - zlo if f else zlo)) for d in range(4) for f in range(2)}
    tops = {(d, f): rows(ys[d] * 2 + (1 - zlo if f else zlo), 0, ROWS // 2)
            for d in range(4) for f in range(2)}
    ends = {(d, f): rows(ys[d] * 2 + (1 - zlo if f else zlo), ROWS // 2, ROWS // 2)
            for d in range(4) for f in range(2)}

    def own(g, name, k):
        ref = g.at[k, slots[0, 0], :]
        start((name, "out"), (name, "pair", k), ref, pair_dev)
        start((name, "out"), (name, "near", 0, k), ref, y_up)
        start((name, "out"), (name, "near", 0, k), ref, y_down)

    def pair(g, name, k):
        ref = g.at[k, slots[0, 1], :]
        arrived((name, "pair", k), ref)
        start((name, "out"), (name, "near", 1, k), ref, y_up)
        start((name, "out"), (name, "near", 1, k), ref, y_down)

    def near(g, name, k, f):
        arrived((name, "near", f, k), g.at[k, 0:2 * ROWS, :])

    def relay(g, name, k, f):
        near(g, name, k, f)
        start((name, "out"), (name, "far", f, k), g.at[k, tops[3, f], :], y_up)
        start((name, "out"), (name, "far", f, k), g.at[k, ends[1, f], :], y_down)

    def far(g, name, k, f):
        arrived((name, "far", f, k), g.at[k, slots[2, f], :])

    def far_pair(g, name, k):
        far(g, name, k, 0)
        start((name, "out"), (name, "far", 1, k), g.at[k, slots[2, 0], :], pair_dev)

    def along_z(q):
        ref = zbuf.at[zhi, :, q * PIECE:(q + 1) * PIECE, :]
        start(("z", "out"), ("z", q), ref, z_up)
        start(("z", "out"), ("z", q), ref, z_down)

    direct = core == lax.div(x, 2)
    depth = {d: pl.ds(pl.multiple_of(zs[d] * WIDE, BLOCK), WIDE) for d in range(4)}
    to_x = [core * 2 + h for h in range(2)]
    home = lax.rem(x, 2)

    def along_x(d, q):
        into = pl.ds(pl.multiple_of(q * BAND + x * PIECE, 16), PIECE)
        dst = lhs.at[into, depth[d]]
        for h in range(2):
            src = zbuf.at[zs[d], h, q * PIECE:(q + 1) * PIECE, :]

            @pl.when(to_x[h] != x)
            def _(h=h, src=src):
                start(("x", "out"), ("x", d, q), src, (r, c + 2 * (to_x[h] - x)), dst)

            @pl.when(to_x[h] == x)
            def _(h=h):
                lhs[into, depth[d]] = zbuf[zs[d], h, q * PIECE:(q + 1) * PIECE, :]

    def relay_z(q):
        arrived(("z", q), zbuf.at[0:2, :, 0:PIECE, :])
        half = PIECE // 2
        for back, row, first in ((3, z_up[0], 0), (1, z_down[0], half)):
            into = pl.ds(pl.multiple_of(q * BAND + x * PIECE + first, 16), half)
            low = q * PIECE + first
            for h in range(2):
                start(("z", "out"), ("x", 2, q), zbuf.at[zs[back], h, low:low + half, :],
                      (row, c + 2 * (to_x[h] - x)), lhs.at[into, depth[back]])

    def to_core(d, q):
        ref = lhs.at[q * BAND:(q + 1) * BAND, depth[d]]

        @pl.when(direct)
        def _():
            arrived(("x", d, q), lhs.at[0:(4 if d == 2 else 3) * PIECE, depth[d]])
            start(("core", "out"), ("core", d, q), ref, core_dev)

    def from_core(d, q):
        @pl.when(jnp.logical_not(direct))
        def _():
            arrived(("core", d, q), lhs.at[q * BAND:(q + 1) * BAND, depth[d]])

    odd_x, odd_z, odd_y = lax.rem(x, 2), lax.rem(zhi, 2), lax.rem(y, 2)

    def step(first, d1, d3):
        return tuple(jnp.where(first, u, v) for u, v in zip(d1, d3))

    trace_to = [
        core_dev, pair_dev,
        step(odd_x == 0, x_dev[1], x_dev[3]), step(odd_x == 1, x_dev[1], x_dev[3]),
        step(odd_y == 0, y_up, y_down), step(odd_y == 1, y_up, y_down),
        step(odd_z == 0, z_up, z_down), step(odd_z == 1, z_up, z_down),
    ]

    def trace_send(i):
        start(("t", "out"), ("t", i), tsend.at[i], trace_to[i], trecv.at[i])

    def trace_sum(i):
        arrived(("t", i), trecv.at[i])
        tsend[i + 1] = tsend[i] + trecv[i]
        if i + 1 < len(trace_to):
            trace_send(i + 1)

    def span(slot):
        return pl.ds(pl.multiple_of(slot * WIDE, BLOCK), WIDE)

    def part_dot(g, k, slot, first=False, band=None):
        band = pl.ds(0, 4 * ROWS) if band is None else band
        term = jnp.dot(lhs[band, span(slot)], g[k, span(slot), :], preferred_element_type=F32)
        acc[k, band] = term if first else acc[k, band] + term

    def piece(k, q, d):
        return acc[k, pl.ds(pl.multiple_of(q * BAND + xs[d] * PIECE, 16), PIECE), :]

    def ship_band(k, q):
        band = pl.ds(q * PIECE, PIECE)
        for d in (2, 1, 3):
            part1[k, d - 1, band] = piece(k, q, d).astype(BF16)
            start(("a", "sums out"), ("a", "sums", k), part1.at[k, d - 1, band, :], x_dev[d],
                  got1.at[k, d - 1, band, :])
        own1[k, band] = piece(k, q, 0)

    def early(q, k):
        band = pl.ds(q * BAND, BAND)
        acc[k, band] = jnp.dot(lhs[band, :], g1[k], preferred_element_type=F32)
        ship_band(k, q)

    def ship(k):
        for d in (2, 1, 3):
            for q in range(NQ):
                part2[k, d - 1, q * PIECE:(q + 1) * PIECE] = piece(k, q, d).astype(BF16)
        for d in (2, 1, 3):
            start(("b", "sums out"), ("b", "sums", k), part2.at[k, d - 1], x_dev[d],
                  got2.at[k, d - 1])
        for q in range(NQ):
            own2[k, q * PIECE:(q + 1) * PIECE] = piece(k, q, 0)

    def total(got, kept, name, k):
        arrived((name, "sums", k), got.at[k])
        return kept[k] + (got[k, 0].astype(F32) + got[k, 2].astype(F32)) + got[k, 1].astype(F32)

    own(g1, "a", 0)
    terms = build(1, terms)
    own(g1, "a", 1)
    terms = build(2, terms)
    own(g1, "a", 2)
    along_z(0)
    along_z(1)
    along_z(2)
    along_x(0, 0)
    along_x(0, 1)
    along_x(0, 2)
    tsend[0] = jnp.sum(terms.reshape(SUB // 8, 8, BLOCK), axis=0)
    trace_send(0)
    pair(g1, "a", 0)
    relay(g1, "a", 0, 0)
    pair(g1, "a", 1)
    relay(g1, "a", 1, 0)
    pair(g1, "a", 2)
    relay(g1, "a", 2, 0)
    relay_z(0)
    along_x(3, 0)
    along_x(1, 0)
    relay(g1, "a", 0, 1)
    relay_z(1)
    along_x(3, 1)
    along_x(1, 1)
    relay(g1, "a", 1, 1)
    relay(g1, "a", 2, 1)
    relay_z(2)
    along_x(3, 2)
    along_x(1, 2)
    for d in (0, 3, 1):
        to_core(d, 0)
    to_core(2, 0)
    far(g1, "a", 0, 0)
    far(g1, "a", 0, 1)
    far(g1, "a", 1, 0)
    far(g1, "a", 1, 1)
    far(g1, "a", 2, 0)
    far(g1, "a", 2, 1)
    for d in (0, 3, 1):
        from_core(d, 0)
    from_core(2, 0)
    for k in range(NCH):
        early(0, k)
    for d in (0, 3, 1):
        to_core(d, 1)
    to_core(2, 1)
    for d in (0, 3, 1):
        from_core(d, 1)
    from_core(2, 1)
    early(1, 0)
    early(1, 1)
    early(1, 2)
    trace_sum(0)
    for d in (0, 3, 1):
        to_core(d, 2)
    for d in (0, 3, 1):
        from_core(d, 2)
    for k in range(NCH):
        for d in (0, 3, 1):
            part_dot(g1, k, zs[d], d == 0, pl.ds(2 * BAND, BAND))
    to_core(2, 2)
    from_core(2, 2)
    for k in range(NCH):
        part_dot(g1, k, zs[2], band=pl.ds(2 * BAND, BAND))
        ship_band(k, 2)
    trace_sum(1)
    def squares(k):
        full = total(got1, own1, "a", k)
        for s in range(ROWS // SUB):
            for h in range(2):
                t = 2 * k + h
                piece = full[s * SUB:(s + 1) * SUB, h * BLOCK:(h + 1) * BLOCK] * keeps[s, t]
                piece = piece.astype(BF16)
                g2[k, rows(me, s * SUB, SUB), h * BLOCK:(h + 1) * BLOCK] = piece
                sq_ref[s * SUB:(s + 1) * SUB, t * BLOCK:(t + 1) * BLOCK] = piece
        own(g2, "b", k)

    squares(0)
    squares(1)
    trace_sum(2)
    pair(g2, "b", 0)
    relay(g2, "b", 0, 0)
    squares(2)
    part_dot(g2, 0, ys[0], True)
    pair(g2, "b", 1)
    relay(g2, "b", 1, 0)
    far_pair(g2, "b", 0)
    trace_sum(3)
    part_dot(g2, 1, ys[0], True)
    pair(g2, "b", 2)
    relay(g2, "b", 2, 0)
    near(g2, "b", 0, 1)
    part_dot(g2, 0, ys[1])
    part_dot(g2, 0, ys[3])
    far_pair(g2, "b", 1)
    trace_sum(4)
    part_dot(g2, 2, ys[0], True)
    far(g2, "b", 0, 1)
    part_dot(g2, 0, ys[2])
    ship(0)
    near(g2, "b", 1, 1)
    part_dot(g2, 1, ys[1])
    part_dot(g2, 1, ys[3])
    far_pair(g2, "b", 2)
    trace_sum(5)
    far(g2, "b", 1, 1)
    part_dot(g2, 1, ys[2])
    ship(1)
    near(g2, "b", 2, 1)
    part_dot(g2, 2, ys[1])
    part_dot(g2, 2, ys[3])
    trace_sum(6)
    far(g2, "b", 2, 1)
    part_dot(g2, 2, ys[2])
    ship(2)
    trace_sum(7)

    trace = jnp.sum(tsend[len(trace_to)], keepdims=True)
    gamma = jnp.sqrt(ORDER / jnp.maximum(jnp.abs(trace), 1.0))
    lead, tail = 1.5 * gamma, 0.5 * gamma * gamma * gamma
    for k in range(NCH):
        cube = total(got2, own2, "b", k)
        for s in range(ROWS // SUB):
            for h in range(2):
                t = 2 * k + h
                piece = cube[s * SUB:(s + 1) * SUB, h * BLOCK:(h + 1) * BLOCK] * keeps[s, t]
                a = g1[k, rows(me, s * SUB, SUB), h * BLOCK:(h + 1) * BLOCK].astype(F32)
                up_ref[s * SUB:(s + 1) * SUB, t * BLOCK:(t + 1) * BLOCK] = (
                    lead * a - tail * piece).astype(BF16)

    sent(("a", "out"), g1.at[:, 0:7 * ROWS, :])
    sent(("b", "out"), g2.at[:, 0:7 * ROWS, :])
    sent(("a", "sums out"), part1)
    sent(("b", "sums out"), part2)
    sent(("z", "out"), zbuf.at[0:3])
    sent(("t", "out"), tsend.at[0:len(trace_to)])

    @pl.when(direct)
    def _():
        sent(("x", "out"), zbuf.at[0:3, 0])
        sent(("core", "out"), lhs)

    @pl.when(jnp.logical_not(direct))
    def _():
        sent(("x", "out"), zbuf.at[0:3])


def publish(sq_ref, up_ref, sq_out, up_out, sems):
    copies = [pltpu.make_async_copy(sq_ref, sq_out, sems.at[0]),
              pltpu.make_async_copy(up_ref, up_out, sems.at[1])]
    for copy in copies:
        copy.start()
    for copy in copies:
        copy.wait()


def body(matrix, pattern, shift):
    block = jax.ShapeDtypeStruct((ROWS, COLS), BF16)
    vmem = pl.BlockSpec(memory_space=pltpu.VMEM)
    hbm = pl.BlockSpec(memory_space=pltpu.HBM)
    results = pl.pallas_call(
        kernel,
        out_shape=(block, block),
        in_specs=[hbm, pl.BlockSpec(memory_space=pltpu.SMEM), hbm],
        out_specs=(vmem, vmem),
        scratch_shapes=[
            pltpu.VMEM((ROWS, COLS), BF16),
            pltpu.VMEM((NBLK, BLOCK), F32),
            pltpu.VMEM((NCH, DEPTH, CHUNK), BF16),
            pltpu.VMEM((NCH, DEPTH, CHUNK), BF16),
            pltpu.VMEM((4, 2, ROWS, WIDE), BF16),
            pltpu.VMEM((4 * ROWS, DEPTH), BF16),
            pltpu.VMEM((NCH, 3, ROWS, CHUNK), BF16),
            pltpu.VMEM((NCH, 3, ROWS, CHUNK), BF16),
            pltpu.VMEM((NCH, 3, ROWS, CHUNK), BF16),
            pltpu.VMEM((NCH, 3, ROWS, CHUNK), BF16),
            pltpu.VMEM((NCH, ROWS, CHUNK), F32),
            pltpu.VMEM((NCH, ROWS, CHUNK), F32),
            pltpu.VMEM((NCH, 4 * ROWS, CHUNK), F32),
            pltpu.VMEM((9, 8, BLOCK), F32),
            pltpu.VMEM((8, 8, BLOCK), F32),
            pltpu.SemaphoreType.DMA((NSEM + 2,)),
        ],
        compiler_params=pltpu.CompilerParams(
            collective_id=0, has_side_effects=True, vmem_limit_bytes=60 * 2**20),
        cost_estimate=pl.CostEstimate(
            flops=4 * ROWS * COLS * ORDER, bytes_accessed=6 * ROWS * COLS, transcendentals=0),
        name="sign_step",
    )(matrix, pattern, shift.reshape(NBLK, BLOCK))
    return pl.pallas_call(
        publish,
        out_shape=(block, block),
        in_specs=[vmem, vmem],
        out_specs=(hbm, hbm),
        scratch_shapes=[pltpu.SemaphoreType.DMA((2,))],
        name="publish",
    )(*results)


def solution(mesh):
    placed = (P("col", "row"), P(), P())
    return jax.shard_map(
        body,
        mesh=mesh,
        in_specs=placed,
        out_specs=(P("col", "row"), P("col", "row")),
        check_vma=False,
    )
```
